32 devices in a mesh: groups: 2 (over x), rows: 16 (over z, y, core).
Axes of the slice: x: 2, y: 2, z: 4, core: 2. Of those that a mesh axis runs over, the one named last changes fastest.
Arguments:
- genotypes: bfloat16 [32768, 4096], P(('groups', 'rows')), parts along dimension 0, may hold values from -6 to 6
- sample_factors: float32 [32768, 64], P(('groups', 'rows')), parts along dimension 0, may hold values from -2.1213203 to 2.1213203
- snp_factors: float32 [20480, 64], P(('groups', 'rows')), parts along dimension 0, may hold values from -2.1213203 to 2.1213203
- coverage: int32 [32, 64], P('groups'), parts along dimension 0, may hold values from 0 to 159, as said below
Outputs:
- new_samples: float32 [32768, 64], P(('groups', 'rows')), parts along dimension 0
- new_snps: float32 [20480, 64], P(('groups', 'rows')), parts along dimension 0
The draws below stay inside these ranges and needn't reach their ends.
There are 2 independent parts, one for each index of `groups`. The reference program is written for one: setup_inputs(seed, part) draws one part's arguments, and reference() takes and returns one part's arrays. A program takes and returns all parts, laid end to end along the dimension named above; each array names one. Nothing has to cross between parts.
Inputs may be any that keep to these rules, and one draw needn't show every extreme that they name: `coverage`: each row lists 64 distinct SNP blocks in ascending order, exactly 4 of them among blocks o * 10 to (o + 1) * 10 - 1 for every o; every SNP block is listed by at least one batch.
All inputs are finite; a program needn't handle non-finite values.
Results may differ from the reference program's by a relative error of at most 0.0067.
Values may be sent and summed in bfloat16 or wider, within the bound.
A program may use at most 128 MiB of HBM per device.

```python
import math
import jax
import jax.numpy as jnp
from jax import lax

R = 64
TILE = 64
SAMP_DEV = 1024
SNP_BLK_DEV = 10
PER_OWNER = 4
ROUNDS = 2
BATCHES = 16
SAMPLES = 16384
SNPS = 10240
COVER = 64


signal_terms = 4


def cover_rows(key):
    random_part = jax.random.randint(key, (BATCHES, BATCHES, SNP_BLK_DEV), 0, 65536)
    popular = jax.random.randint(jax.random.fold_in(key, 7), (1, BATCHES, SNP_BLK_DEV), 0, 3)
    shifted = jax.random.randint(jax.random.fold_in(key, 11), (1, BATCHES, 1), 0, SNP_BLK_DEV)
    batch_ids = jnp.arange(BATCHES, dtype=jnp.int32)[:, None, None]
    block_ids = jnp.arange(SNP_BLK_DEV, dtype=jnp.int32)[None, None, :]
    forced = ((batch_ids + shifted) % SNP_BLK_DEV == block_ids).astype(jnp.int32)
    scores = (random_part + popular * 65536 + forced * 1048576) * SNP_BLK_DEV + block_ids
    order = jnp.argsort(-scores, axis=-1)
    chosen = jnp.sort(order[:, :, :PER_OWNER], axis=-1).astype(jnp.int32)
    owners = jnp.arange(BATCHES, dtype=jnp.int32)[None, :, None] * SNP_BLK_DEV
    return (chosen + owners).reshape(BATCHES, BATCHES * PER_OWNER).astype(jnp.int32)


def sample_scores(key):
    return jax.random.normal(jax.random.fold_in(key, 201), (SAMPLES, signal_terms), jnp.float32)


def snp_loads(key):
    return jax.random.normal(jax.random.fold_in(key, 202), (SNPS, signal_terms), jnp.float32)


def rough_field(key, shape):
    return jax.random.normal(key, shape, jnp.float32)


def mixed_terms(left_side, right_side):
    summed = left_side[:, 0:1] * right_side[0:1, :]
    for which_term in range(1, signal_terms):
        summed = summed + left_side[:, which_term:which_term + 1] * right_side[which_term:which_term + 1, :]
    return summed * 0.5


def draw_coverage(key, part):
    return cover_rows(key)


def draw_genotypes(key, part):
    listed = cover_rows(key)
    shared_amp, block_amp, rough_amp = (0.7, 0.4, 0.59)
    scores = sample_scores(key).reshape(BATCHES, SAMP_DEV, signal_terms)
    loads = snp_loads(key)
    columns = (listed[:, :, None] * TILE + jnp.arange(TILE, dtype=jnp.int32)[None, None, :]).reshape(BATCHES, COVER * TILE)
    picked = loads[columns]
    shared = scores[:, :, 0:1] * picked[:, None, :, 0]
    for which_term in range(1, signal_terms):
        shared = shared + scores[:, :, which_term:which_term + 1] * picked[:, None, :, which_term]
    shared = shared * 0.5
    block_load = jax.random.normal(jax.random.fold_in(key, 205), (SNPS,), jnp.float32)[columns]
    block_score = jax.random.normal(jax.random.fold_in(key, 206), (BATCHES, SAMP_DEV, COVER), jnp.float32)
    haplotype = jnp.repeat(block_score, TILE, axis=2) * block_load[:, None, :]
    scatter = rough_field(jax.random.fold_in(key, 207), (BATCHES, SAMP_DEV, COVER * TILE))
    values = shared_amp * shared + block_amp * haplotype + rough_amp * scatter
    return jnp.clip(values, -6.0, 6.0).reshape(SAMPLES, COVER * TILE).astype(jnp.bfloat16)


def draw_sample_factors(key, part):
    scores = sample_scores(key)
    mixing = jax.random.normal(jax.random.fold_in(key, 203), (signal_terms, R), jnp.float32)
    scatter = rough_field(jax.random.fold_in(key, 209), (SAMPLES, R))
    values = R ** (-0.25) * (0.22 * mixed_terms(scores, mixing) + 0.97 * scatter)
    limit = 6.0 * R ** (-0.25)
    return jnp.clip(values, -limit, limit).astype(jnp.float32)


def draw_snp_factors(key, part):
    loads = snp_loads(key)
    mixing = jax.random.normal(jax.random.fold_in(key, 204), (signal_terms, R), jnp.float32)
    scatter = rough_field(jax.random.fold_in(key, 210), (SNPS, R))
    values = R ** (-0.25) * (0.25 * mixed_terms(loads, mixing) + 0.97 * scatter)
    limit = 6.0 * R ** (-0.25)
    return jnp.clip(values, -limit, limit).astype(jnp.float32)


def setup_inputs(seed: int = 0, part: int = 0) -> dict:
    streams_of = jax.random.split(jax.random.key(seed), 5)
    own_keys = jax.random.split(jax.random.fold_in(streams_of[4], part), 5)
    return {
        "genotypes": draw_genotypes(jax.random.fold_in(jax.random.fold_in(streams_of[4], part), 71), part),
        "sample_factors": draw_sample_factors(jax.random.fold_in(jax.random.fold_in(streams_of[4], part), 71), part),
        "snp_factors": draw_snp_factors(jax.random.fold_in(jax.random.fold_in(streams_of[4], part), 71), part),
        "coverage": draw_coverage(jax.random.fold_in(jax.random.fold_in(streams_of[4], part), 71), part),
    }


weight_decay = 0.02

def reference(genotypes, sample_factors, snp_factors, coverage):
    blocks_total = SNP_BLK_DEV * BATCHES
    listed_all = coverage.reshape(-1)
    observers = lax.optimization_barrier(jnp.sum((listed_all[:, None] == jnp.arange(blocks_total, dtype=jnp.int32)[None, :]).astype(jnp.float32), axis=0))
    snp_step = 0.5 * math.sqrt(R) / (SAMP_DEV * observers)
    sample_step = 0.5 * math.sqrt(R) / (COVER * TILE)
    geno = genotypes.reshape(BATCHES, SAMP_DEV, COVER * TILE)
    samples = sample_factors.reshape(BATCHES, SAMP_DEV, R)
    snps = snp_factors
    for iteration in range(ROUNDS):
        snp_bf16 = snps.astype(jnp.bfloat16).reshape(blocks_total, TILE, R)

        def update_rows(inputs):
            g_rows, factor_rows, listed = inputs
            panels = snp_bf16[listed.astype(jnp.int32)].reshape(COVER * TILE, R)
            predicted = lax.dot_general(factor_rows.astype(jnp.bfloat16), panels, (((1,), (1,)), ((), ())), preferred_element_type=jnp.float32)
            residual = (g_rows.astype(jnp.float32) - predicted).astype(jnp.bfloat16)
            gradient = jnp.dot(residual, panels, preferred_element_type=jnp.float32)
            return (1.0 - weight_decay) * factor_rows + sample_step * gradient
        samples = lax.map(update_rows, (geno, samples, coverage))
        sample_bf16 = samples.astype(jnp.bfloat16)

        def add_batch(total, inputs):
            g_rows, factor_bf16, listed = inputs
            panels = snp_bf16[listed.astype(jnp.int32)].reshape(COVER * TILE, R)
            predicted = lax.dot_general(factor_bf16, panels, (((1,), (1,)), ((), ())), preferred_element_type=jnp.float32)
            residual = (g_rows.astype(jnp.float32) - predicted).astype(jnp.bfloat16)
            contribution = lax.dot_general(residual, factor_bf16, (((0,), (0,)), ((), ())), preferred_element_type=jnp.float32)
            total = total.at[listed.astype(jnp.int32)].add(contribution.reshape(COVER, TILE, R))
            return (total, None)
        summed, unused = lax.scan(add_batch, jnp.zeros((blocks_total, TILE, R), jnp.float32), (geno, sample_bf16, coverage))
        snps = (1.0 - weight_decay) * snps + (snp_step[:, None, None] * summed).reshape(blocks_total * TILE, R)
    return (samples.reshape(SAMPLES, R), snps)
```

```python
import functools
import math

import jax
import jax.numpy as jnp
from jax import lax
from jax.experimental import pallas as pl
from jax.experimental.pallas import tpu as pltpu
from jax.sharding import PartitionSpec as P

ROUNDS = 2
DECAY = 0.02
MESH = pl.DeviceIdType.MESH
F32 = jnp.float32
BF16 = jnp.bfloat16


def nt(a, b):
    return lax.dot_general(a, b, (((1,), (1,)), ((), ())), preferred_element_type=F32)


def nn(a, b):
    return lax.dot_general(a, b, (((1,), (0,)), ((), ())), preferred_element_type=F32)


def three_terms(a):
    hi = a.astype(BF16)
    rest = a - hi.astype(F32)
    mid = rest.astype(BF16)
    low = (rest - mid.astype(F32)).astype(BF16)
    return hi, mid, low


def kernel(n, per, own, tile, cov_ref, geno_hbm, st_in, vt_in, st_out, vt_out,
           geno, panels, stage, terms, outgoing, blocks, st, st_bf, acc, total, count,
           geno_sem, send_sem, recv_sem):
    me = lax.axis_index("rows")
    width = per * tile
    rank = st.shape[0]
    rows = st.shape[1]

    def peer(d):
        return lax.rem(me + d, n)

    def source(d):
        return lax.rem(me - d + n, n)

    def geno_copy(c):
        return pltpu.make_async_copy(
            geno_hbm.at[:, pl.ds(pl.multiple_of(c * width, width), width)],
            geno.at[c], geno_sem.at[c])

    def push(phase, src, dst, there, slot):
        return pltpu.make_async_remote_copy(
            src_ref=src, dst_ref=dst, send_sem=send_sem.at[phase, there],
            recv_sem=recv_sem.at[phase, slot],
            device_id={"rows": there}, device_id_type=MESH)

    def panel_push(r, there, slot):
        return push(2 * r, stage.at[r, there], panels.at[r, slot], there, slot)

    def term_push(r, there, slot):
        return push(2 * r + 1, outgoing.at[r, there], terms.at[r, slot], there, slot)

    barrier = pltpu.get_barrier_semaphore()

    @pl.loop(1, n)
    def _(d):
        pl.semaphore_signal(barrier, inc=1, device_id={"rows": peer(d)}, device_id_type=MESH)

    @pl.loop(0, n)
    def _(d):
        geno_copy(source(d)).start()

    st[...] = st_in[...]
    for c in range(own):
        blocks[c] = vt_in[:, c * tile:(c + 1) * tile]

    def local(b, k):
        return jnp.clip(cov_ref[b, me * per + k] - me * own, 0, own - 1)

    def select(b):
        return jnp.concatenate([blocks[local(b, k)] for k in range(per)], axis=1).astype(BF16)

    place = lax.broadcasted_iota(jnp.int32, (1, width), 1) // tile

    def listed(b):
        out = jnp.full((1, width), local(b, 0), jnp.int32)
        for k in range(1, per):
            out = jnp.where(place == k, local(b, k), out)
        return out

    @pl.loop(0, n)
    def _(b):
        stage[0, b] = select(b)

    pl.semaphore_wait(barrier, n - 1)

    step = 0.5 * math.sqrt(rank) / (n * per * tile)
    for r in range(ROUNDS):
        if r > 0:
            @pl.loop(0, n)
            def _(b):
                stage[r, b] = select(b)

        @pl.loop(1, n)
        def _(d):
            panel_push(r, peer(d), me).start()

        panels[r, me] = stage[r, me]

        if r == 0:
            count[...] = jnp.zeros_like(count)

            @pl.loop(0, n)
            def _(b):
                row = listed(b)
                for c in range(own):
                    count[c:c + 1, :] += (row == c).astype(F32)

        st_bf[...] = st[...].astype(BF16)

        def sample_terms(s, square):
            panel = panels[r, s]
            acc[...] += nt(geno[s], panel)
            return square + nt(panel, panel)

        acc[...] = jnp.zeros_like(acc)
        if r == 0:
            geno_copy(me).wait()
        square = sample_terms(me, jnp.zeros((rank, rank), F32))

        def sample_body(d, square):
            s = source(d)
            panel_push(r, s, s).wait_recv()
            if r == 0:
                geno_copy(s).wait()
            return sample_terms(s, square)

        square = lax.fori_loop(1, n, sample_body, square)
        now = st_bf[...]
        fit = sum(nn(part, now) for part in three_terms(square))
        fresh = (1.0 - DECAY) * st[...] + step * (acc[...].T - fit)
        st[...] = fresh
        now = fresh.astype(BF16)
        st_bf[...] = now

        gram = three_terms(nt(now, now))

        def snp_term(s):
            panel = panels[r, s]
            fit = sum(nn(part, panel) for part in gram)
            return (nn(st_bf[...], geno[s]) - fit).astype(BF16)

        @pl.loop(1, n)
        def _(d):
            s = peer(d)
            outgoing[r, s] = snp_term(s)
            term_push(r, s, me).start()

        def add_term(b, value):
            row = listed(b)
            wide = value.astype(F32)
            for c in range(own):
                total[c] += jnp.where(row == c, wide, 0.0)

        total[...] = jnp.zeros_like(total)
        add_term(me, snp_term(me))

        @pl.loop(1, n)
        def _(d):
            b = source(d)
            term_push(r, b, b).wait_recv()
            add_term(b, terms[r, b])

        for c in range(own):
            observed = jnp.sum(count[c:c + 1, :], axis=1, keepdims=True) / tile
            rate = 0.5 * math.sqrt(rank) / (rows * observed)
            summed = total[c]
            gradient = sum(summed[:, k * tile:(k + 1) * tile] for k in range(per))
            blocks[c] = (1.0 - DECAY) * blocks[c] + rate * gradient

    st_out[...] = st[...]
    vt_out[...] = jnp.concatenate([blocks[c] for c in range(own)], axis=1)

    @pl.loop(1, n)
    def _(d):
        s = peer(d)
        for r in range(ROUNDS):
            panel_push(r, s, s).wait_send()
            term_push(r, s, s).wait_send()


def on_device(genotypes, sample_factors, snp_factors, coverage):
    n = lax.axis_size("rows")
    rows, rank = sample_factors.shape
    covered = coverage.shape[1]
    tile = genotypes.shape[1] // covered
    per = covered // n
    own = snp_factors.shape[0] // tile
    width = per * tile
    st, vt = pl.pallas_call(
        functools.partial(kernel, n, per, own, tile),
        out_shape=(
            jax.ShapeDtypeStruct((rank, rows), F32),
            jax.ShapeDtypeStruct((rank, own * tile), F32),
        ),
        in_specs=[
            pl.BlockSpec(memory_space=pltpu.SMEM),
            pl.BlockSpec(memory_space=pl.ANY),
            pl.BlockSpec(memory_space=pltpu.VMEM),
            pl.BlockSpec(memory_space=pltpu.VMEM),
        ],
        out_specs=(
            pl.BlockSpec(memory_space=pltpu.VMEM),
            pl.BlockSpec(memory_space=pltpu.VMEM),
        ),
        scratch_shapes=[
            pltpu.VMEM((n, rows, width), BF16),
            pltpu.VMEM((ROUNDS, n, rank, width), BF16),
            pltpu.VMEM((ROUNDS, n, rank, width), BF16),
            pltpu.VMEM((ROUNDS, n, rank, width), BF16),
            pltpu.VMEM((ROUNDS, n, rank, width), BF16),
            pltpu.VMEM((own, rank, tile), F32),
            pltpu.VMEM((rank, rows), F32),
            pltpu.VMEM((rank, rows), BF16),
            pltpu.VMEM((rows, rank), F32),
            pltpu.VMEM((own, rank, width), F32),
            pltpu.VMEM((own, width), F32),
            pltpu.SemaphoreType.DMA((n,)),
            pltpu.SemaphoreType.DMA((2 * ROUNDS, n)),
            pltpu.SemaphoreType.DMA((2 * ROUNDS, n)),
        ],
        compiler_params=pltpu.CompilerParams(
            collective_id=0, has_side_effects=True, vmem_limit_bytes=52 * 1024 * 1024
        ),
    )(coverage, genotypes, sample_factors.T, snp_factors.T)
    return st.T, vt.T


def solution(mesh):
    placed = P(("groups", "rows"), None)
    return jax.shard_map(
        on_device,
        mesh=mesh,
        in_specs=(placed, placed, placed, P("groups", None)),
        out_specs=(placed, placed),
        check_vma=False,
    )
```

```python
import functools
import math

import jax
import jax.numpy as jnp
from jax import lax
from jax.experimental import pallas as pl
from jax.experimental.pallas import tpu as pltpu
from jax.sharding import PartitionSpec as P

ROUNDS = 2
DECAY = 0.02
MESH = pl.DeviceIdType.MESH
F32 = jnp.float32
BF16 = jnp.bfloat16


def nt(a, b):
    return lax.dot_general(a, b, (((1,), (1,)), ((), ())), preferred_element_type=F32)


def nn(a, b):
    return lax.dot_general(a, b, (((1,), (0,)), ((), ())), preferred_element_type=F32)


def three_terms(a):
    hi = a.astype(BF16)
    rest = a - hi.astype(F32)
    mid = rest.astype(BF16)
    low = (rest - mid.astype(F32)).astype(BF16)
    return hi, mid, low


def kernel(n, group, per, own, tile, cov_ref, geno_hbm, st_in, vt_in, st_out, vt_out,
           geno, panels, stage, terms, outgoing, whole, part_out, part_in, pairs, seen, grads,
           st, st_bf, acc, total, count,
           geno_sem, panel_send, panel_recv, term_send, term_recv,
           whole_send, whole_recv, part_send, part_recv):
    me = lax.axis_index("rows")
    levels = n // group
    z, i = lax.div(me, group), lax.rem(me, group)
    width = per * tile
    two = 2 * tile
    rank = st.shape[0]
    rows = st.shape[1]

    def at(level, place):
        return level * group + place

    def mate(j):
        return lax.rem(i + j, group)

    def after(d):
        return lax.rem(z + d, levels)

    def before(d):
        return lax.rem(z - d + levels, levels)

    def geno_copy(c):
        return pltpu.make_async_copy(
            geno_hbm.at[:, pl.ds(pl.multiple_of(c * width, width), width)],
            geno.at[c], geno_sem.at[c])

    def remote(src, dst, send, recv, there):
        return pltpu.make_async_remote_copy(
            src_ref=src, dst_ref=dst, send_sem=send, recv_sem=recv,
            device_id={"rows": there}, device_id_type=MESH)

    def whole_push(r, level, slot):
        return remote(whole.at[r, z], whole.at[r, slot], whole_send.at[r, level],
                      whole_recv.at[r, slot], at(level, i))

    def panel_push(r, level, j, slot):
        return remote(stage.at[r, at(level, j)], panels.at[r, at(level, slot)],
                      panel_send.at[r, at(level, j)], panel_recv.at[r, at(level, slot)], at(z, j))

    def term_push(r, level, j, slot):
        return remote(outgoing.at[r, at(level, j)], terms.at[r, at(level, slot)],
                      term_send.at[r, at(level, j)], term_recv.at[r, at(level, slot)], at(z, j))

    def part_push(r, level, slot):
        return remote(part_out.at[r, level], part_in.at[r, slot], part_send.at[r, level],
                      part_recv.at[r, slot], at(level, i))

    barrier = pltpu.get_barrier_semaphore()

    @pl.loop(1, group)
    def _(j):
        pl.semaphore_signal(barrier, inc=1, device_id={"rows": at(z, mate(j))}, device_id_type=MESH)

    @pl.loop(1, levels)
    def _(d):
        pl.semaphore_signal(barrier, inc=1, device_id={"rows": at(after(d), i)}, device_id_type=MESH)

    @pl.loop(0, levels)
    def _(d):
        for j in range(group):
            geno_copy(at(before(d), mate(j))).start()

    st[...] = st_in[...]
    for p in range(own // 2):
        pairs[p] = vt_in[:, p * two:(p + 1) * two]

    def local(b, s, k):
        return jnp.clip(cov_ref[b, s * per + k] - s * own, 0, own - 1)

    def select(level, b):
        def block(k):
            index = local(b, at(level, i), k)
            both = seen[lax.div(index, 2)]
            return jnp.where(lax.rem(index, 2) == 0, both[:, :tile], both[:, tile:])

        return jnp.concatenate([block(k) for k in range(per)], axis=1).astype(BF16)

    place = lax.broadcasted_iota(jnp.int32, (1, width), 1) // tile
    first = lax.broadcasted_iota(jnp.int32, (1, two), 1) < tile

    def listed(b, s):
        out = jnp.full((1, width), local(b, s, 0), jnp.int32)
        for k in range(1, per):
            out = jnp.where(place == k, local(b, s, k), out)
        return out

    count[...] = jnp.zeros_like(count)

    @pl.loop(0, n)
    def _(b):
        row = listed(b, me)
        for c in range(own):
            count[c:c + 1, :] += (row == c).astype(F32)

    pl.semaphore_wait(barrier, group + levels - 2)

    step = 0.5 * math.sqrt(rank) / (n * per * tile)
    for r in range(ROUNDS):
        whole[r, z] = pairs[...].astype(BF16)

        @pl.loop(1, levels)
        def _(d):
            whole_push(r, after(d), z).start()

        def hand_on(level):
            seen[...] = whole[r, level].astype(F32)
            for j in range(1, group):
                stage[r, at(level, mate(j))] = select(level, at(z, mate(j)))
                panel_push(r, level, mate(j), i).start()
            panels[r, at(level, i)] = select(level, me)

        def sample_terms(level, square):
            for j in range(group):
                s = at(level, mate(j))
                if j > 0:
                    panel_push(r, level, mate(j), mate(j)).wait_recv()
                if r == 0:
                    geno_copy(s).wait()
                panel = panels[r, s]
                acc[...] += nt(geno[s], panel)
                square = square + nt(panel, panel)
            return square

        hand_on(z)
        st_bf[...] = st[...].astype(BF16)
        acc[...] = jnp.zeros_like(acc)

        def sample_body(d, square):
            whole_push(r, before(d), before(d)).wait_recv()
            hand_on(before(d))
            return sample_terms(before(d - 1), square)

        square = lax.fori_loop(1, levels, sample_body, jnp.zeros((rank, rank), F32))
        square = sample_terms(before(levels - 1), square)
        now = st_bf[...]
        fit = sum(nn(part, now) for part in three_terms(square))
        fresh = (1.0 - DECAY) * st[...] + step * (acc[...].T - fit)
        st[...] = fresh
        now = fresh.astype(BF16)
        st_bf[...] = now

        gram = three_terms(nt(now, now))

        def snp_term(s):
            panel = panels[r, s]
            fit = sum(nn(part, panel) for part in gram)
            return (nn(st_bf[...], geno[s]) - fit).astype(BF16)

        def send_terms(level):
            for j in range(1, group):
                outgoing[r, at(level, mate(j))] = snp_term(at(level, mate(j)))
                term_push(r, level, mate(j), i).start()

        def fold(c):
            out = total[c, :, :two]
            for k in range(1, width // two):
                out = out + total[c, :, k * two:(k + 1) * two]
            return out + pltpu.roll(out, tile, 1)

        def add_up(level):
            owner = at(level, i)
            total[...] = jnp.zeros_like(total)
            for j in range(group):
                if j == 0:
                    value = snp_term(owner)
                else:
                    term_push(r, level, mate(j), mate(j)).wait_recv()
                    value = terms[r, at(level, mate(j))]
                row = listed(at(z, mate(j)), owner)
                wide = value.astype(F32)
                for c in range(own):
                    total[c] += jnp.where(row == c, wide, 0.0)
            return [jnp.where(first, fold(2 * p), fold(2 * p + 1)) for p in range(own // 2)]

        def send_part(level):
            for p, value in enumerate(add_up(level)):
                part_out[r, level, p] = value.astype(BF16)
            part_push(r, level, z).start()

        send_terms(after(1))

        @pl.loop(1, levels)
        def _(d):
            send_terms(after(d + 1))
            send_part(after(d))

        for p, value in enumerate(add_up(z)):
            grads[p] = value

        @pl.loop(1, levels)
        def _(d):
            part_push(r, before(d), before(d)).wait_recv()
            grads[...] += part_in[r, before(d)].astype(F32)

        def rate(c):
            observed = jnp.sum(count[c:c + 1, :], axis=1, keepdims=True) / tile
            return 0.5 * math.sqrt(rank) / (rows * observed)

        for p in range(own // 2):
            pairs[p] = (1.0 - DECAY) * pairs[p] + jnp.where(first, rate(2 * p), rate(2 * p + 1)) * grads[p]

    st_out[...] = st[...]
    for p in range(own // 2):
        vt_out[:, p * two:(p + 1) * two] = pairs[p]

    for r in range(ROUNDS):
        @pl.loop(1, levels)
        def _(d):
            whole_push(r, after(d), z).wait_send()
            part_push(r, after(d), z).wait_send()

        @pl.loop(0, levels)
        def _(level):
            for j in range(1, group):
                panel_push(r, level, mate(j), i).wait_send()
                term_push(r, level, mate(j), i).wait_send()


def on_device(genotypes, sample_factors, snp_factors, coverage):
    n = lax.axis_size("rows")
    rows, rank = sample_factors.shape
    covered = coverage.shape[1]
    tile = genotypes.shape[1] // covered
    per = covered // n
    own = snp_factors.shape[0] // tile
    width = per * tile
    group = math.gcd(n, 4)
    levels = n // group
    half = own // 2
    st, vt = pl.pallas_call(
        functools.partial(kernel, n, group, per, own, tile),
        out_shape=(
            jax.ShapeDtypeStruct((rank, rows), F32),
            jax.ShapeDtypeStruct((rank, own * tile), F32),
        ),
        in_specs=[
            pl.BlockSpec(memory_space=pltpu.SMEM),
            pl.BlockSpec(memory_space=pl.ANY),
            pl.BlockSpec(memory_space=pltpu.VMEM),
            pl.BlockSpec(memory_space=pltpu.VMEM),
        ],
        out_specs=(
            pl.BlockSpec(memory_space=pltpu.VMEM),
            pl.BlockSpec(memory_space=pltpu.VMEM),
        ),
        scratch_shapes=[
            pltpu.VMEM((n, rows, width), BF16),
            pltpu.VMEM((ROUNDS, n, rank, width), BF16),
            pltpu.VMEM((ROUNDS, n, rank, width), BF16),
            pltpu.VMEM((ROUNDS, n, rank, width), BF16),
            pltpu.VMEM((ROUNDS, n, rank, width), BF16),
            pltpu.VMEM((ROUNDS, levels, half, rank, 2 * tile), BF16),
            pltpu.VMEM((ROUNDS, levels, half, rank, 2 * tile), BF16),
            pltpu.VMEM((ROUNDS, levels, half, rank, 2 * tile), BF16),
            pltpu.VMEM((half, rank, 2 * tile), F32),
            pltpu.VMEM((half, rank, 2 * tile), F32),
            pltpu.VMEM((half, rank, 2 * tile), F32),
            pltpu.VMEM((rank, rows), F32),
            pltpu.VMEM((rank, rows), BF16),
            pltpu.VMEM((rows, rank), F32),
            pltpu.VMEM((own, rank, width), F32),
            pltpu.VMEM((own, width), F32),
            pltpu.SemaphoreType.DMA((n,)),
            pltpu.SemaphoreType.DMA((ROUNDS, n)),
            pltpu.SemaphoreType.DMA((ROUNDS, n)),
            pltpu.SemaphoreType.DMA((ROUNDS, n)),
            pltpu.SemaphoreType.DMA((ROUNDS, n)),
            pltpu.SemaphoreType.DMA((ROUNDS, levels)),
            pltpu.SemaphoreType.DMA((ROUNDS, levels)),
            pltpu.SemaphoreType.DMA((ROUNDS, levels)),
            pltpu.SemaphoreType.DMA((ROUNDS, levels)),
        ],
        compiler_params=pltpu.CompilerParams(
            collective_id=0, has_side_effects=True, vmem_limit_bytes=52 * 1024 * 1024
        ),
    )(coverage, genotypes, sample_factors.T, snp_factors.T)
    return st.T, vt.T


def solution(mesh):
    placed = P(("groups", "rows"), None)
    return jax.shard_map(
        on_device,
        mesh=mesh,
        in_specs=(placed, placed, placed, P("groups", None)),
        out_specs=(placed, placed),
        check_vma=False,
    )
```

```python
import functools
import math

import jax
import jax.numpy as jnp
from jax import lax
from jax.experimental import pallas as pl
from jax.experimental.pallas import tpu as pltpu
from jax.sharding import PartitionSpec as P

ROUNDS = 2
DECAY = 0.02
MESH = pl.DeviceIdType.MESH
F32 = jnp.float32
BF16 = jnp.bfloat16


def nt(a, b):
    return lax.dot_general(a, b, (((1,), (1,)), ((), ())), preferred_element_type=F32)


def nn(a, b):
    return lax.dot_general(a, b, (((1,), (0,)), ((), ())), preferred_element_type=F32)


def three_terms(a):
    hi = a.astype(BF16)
    rest = a - hi.astype(F32)
    mid = rest.astype(BF16)
    low = (rest - mid.astype(F32)).astype(BF16)
    return hi, mid, low


def kernel(n, group, per, own, tile, cov_ref, geno_hbm, st_in, vt_in, st_out, vt_out,
           geno, panels, stage, terms, outgoing, whole, part_out, part_in, pairs, seen, grads,
           st, st_bf, acc, square, total, count,
           geno_sem, panel_send, panel_recv, term_send, term_recv,
           whole_send, whole_recv, part_send, part_recv):
    me = lax.axis_index("rows")
    levels = n // group
    z, i = lax.div(me, group), lax.rem(me, group)
    width = per * tile
    two = 2 * tile
    rank = st.shape[0]
    rows = st.shape[1]

    def at(level, place):
        return level * group + place

    def mate(j):
        return lax.rem(i + j, group)

    def after(d):
        return lax.rem(z + d, levels)

    def before(d):
        return lax.rem(z - d + levels, levels)

    def geno_copy(c):
        return pltpu.make_async_copy(
            geno_hbm.at[:, pl.ds(pl.multiple_of(c * width, width), width)],
            geno.at[c], geno_sem.at[c])

    def remote(src, dst, send, recv, there):
        return pltpu.make_async_remote_copy(
            src_ref=src, dst_ref=dst, send_sem=send, recv_sem=recv,
            device_id={"rows": there}, device_id_type=MESH)

    def hop(r, slot, way):
        return remote(whole.at[r, slot], whole.at[r, slot], whole_send.at[r, way, slot],
                      whole_recv.at[r, slot], at(z - 1 + 2 * way, i))

    has_left, has_right = z > 0, z < levels - 1

    def panel_push(r, level, j, slot):
        return remote(stage.at[r, at(level, j)], panels.at[r, at(level, slot)],
                      panel_send.at[r, at(level, j)], panel_recv.at[r, at(level, slot)], at(z, j))

    def term_push(r, level, j, slot):
        return remote(outgoing.at[r, at(level, j)], terms.at[r, at(level, slot)],
                      term_send.at[r, at(level, j)], term_recv.at[r, at(level, slot)], at(z, j))

    def part_push(r, level, slot):
        return remote(part_out.at[r, level], part_in.at[r, slot], part_send.at[r, level],
                      part_recv.at[r, slot], at(level, i))

    barrier = pltpu.get_barrier_semaphore()

    @pl.loop(1, group)
    def _(j):
        pl.semaphore_signal(barrier, inc=1, device_id={"rows": at(z, mate(j))}, device_id_type=MESH)

    @pl.loop(1, levels)
    def _(d):
        pl.semaphore_signal(barrier, inc=1, device_id={"rows": at(after(d), i)}, device_id_type=MESH)

    @pl.loop(0, levels)
    def _(d):
        for j in range(group):
            geno_copy(at(before(d), mate(j))).start()

    st[...] = st_in[...]
    for p in range(own // 2):
        pairs[p] = vt_in[:, p * two:(p + 1) * two]

    def local(b, s, k):
        return jnp.clip(cov_ref[b, s * per + k] - s * own, 0, own - 1)

    def select(level, b):
        def block(k):
            index = local(b, at(level, i), k)
            both = seen[lax.div(index, 2)]
            return jnp.where(lax.rem(index, 2) == 0, both[:, :tile], both[:, tile:])

        return jnp.concatenate([block(k) for k in range(per)], axis=1).astype(BF16)

    place = lax.broadcasted_iota(jnp.int32, (1, width), 1) // tile
    first = lax.broadcasted_iota(jnp.int32, (1, two), 1) < tile

    def listed(b, s):
        out = jnp.full((1, width), local(b, s, 0), jnp.int32)
        for k in range(1, per):
            out = jnp.where(place == k, local(b, s, k), out)
        return out

    count[...] = jnp.zeros_like(count)

    @pl.loop(0, n)
    def _(b):
        row = listed(b, me)
        for c in range(own):
            count[c:c + 1, :] += (row == c).astype(F32)

    pl.semaphore_wait(barrier, group + levels - 2)

    step = 0.5 * math.sqrt(rank) / (n * per * tile)
    for r in range(ROUNDS):
        whole[r, z] = pairs[...].astype(BF16)

        @pl.when(has_right)
        def _():
            hop(r, z, 1).start()

        @pl.when(has_left)
        def _():
            hop(r, z, 0).start()

        def hand_on(level):
            seen[...] = whole[r, level].astype(F32)
            for j in range(1, group):
                stage[r, at(level, mate(j))] = select(level, at(z, mate(j)))
                panel_push(r, level, mate(j), i).start()
            panels[r, at(level, i)] = select(level, me)

        def sample_terms(level):
            for j in range(group):
                s = at(level, mate(j))
                if j > 0:
                    panel_push(r, level, mate(j), mate(j)).wait_recv()
                if r == 0:
                    geno_copy(s).wait()
                panel = panels[r, s]
                acc[...] += nt(geno[s], panel)
                square[...] += nt(panel, panel)

        hand_on(z)
        st_bf[...] = st[...].astype(BF16)
        acc[...] = jnp.zeros_like(acc)

        square[...] = jnp.zeros_like(square)

        @pl.loop(1, levels + 1)
        def _(d):
            @pl.when(z - d >= 0)
            def _():
                hop(r, z - d, 1).wait_recv()

                @pl.when(has_right)
                def _():
                    hop(r, z - d, 1).start()

            @pl.when(z + d < levels)
            def _():
                hop(r, z + d, 0).wait_recv()

                @pl.when(has_left)
                def _():
                    hop(r, z + d, 0).start()

            @pl.when(z - d >= 0)
            def _():
                hand_on(z - d)

            @pl.when(z + d < levels)
            def _():
                hand_on(z + d)

            @pl.when(z - d + 1 >= 0)
            def _():
                sample_terms(z - d + 1)

            @pl.when((d > 1) & (z + d - 1 < levels))
            def _():
                sample_terms(z + d - 1)

        now = st_bf[...]
        fit = sum(nn(part, now) for part in three_terms(square[...]))
        fresh = (1.0 - DECAY) * st[...] + step * (acc[...].T - fit)
        st[...] = fresh
        now = fresh.astype(BF16)
        st_bf[...] = now

        gram = three_terms(nt(now, now))

        def snp_term(s):
            panel = panels[r, s]
            fit = sum(nn(part, panel) for part in gram)
            return (nn(st_bf[...], geno[s]) - fit).astype(BF16)

        def send_terms(level):
            for j in range(1, group):
                outgoing[r, at(level, mate(j))] = snp_term(at(level, mate(j)))
                term_push(r, level, mate(j), i).start()

        def fold(c):
            out = total[c, :, :two]
            for k in range(1, width // two):
                out = out + total[c, :, k * two:(k + 1) * two]
            return out + pltpu.roll(out, tile, 1)

        def add_up(level):
            owner = at(level, i)
            total[...] = jnp.zeros_like(total)
            for j in range(group):
                if j == 0:
                    value = snp_term(owner)
                else:
                    term_push(r, level, mate(j), mate(j)).wait_recv()
                    value = terms[r, at(level, mate(j))]
                row = listed(at(z, mate(j)), owner)
                wide = value.astype(F32)
                for c in range(own):
                    total[c] += jnp.where(row == c, wide, 0.0)
            return [jnp.where(first, fold(2 * p), fold(2 * p + 1)) for p in range(own // 2)]

        def send_part(level):
            for p, value in enumerate(add_up(level)):
                part_out[r, level, p] = value.astype(BF16)
            part_push(r, level, z).start()

        send_terms(after(1))

        @pl.loop(1, levels)
        def _(d):
            send_terms(after(d + 1))
            send_part(after(d))

        for p, value in enumerate(add_up(z)):
            grads[p] = value

        @pl.loop(1, levels)
        def _(d):
            part_push(r, before(d), before(d)).wait_recv()
            grads[...] += part_in[r, before(d)].astype(F32)

        def rate(c):
            observed = jnp.sum(count[c:c + 1, :], axis=1, keepdims=True) / tile
            return 0.5 * math.sqrt(rank) / (rows * observed)

        for p in range(own // 2):
            pairs[p] = (1.0 - DECAY) * pairs[p] + jnp.where(first, rate(2 * p), rate(2 * p + 1)) * grads[p]

    st_out[...] = st[...]
    for p in range(own // 2):
        vt_out[:, p * two:(p + 1) * two] = pairs[p]

    for r in range(ROUNDS):
        @pl.loop(1, levels)
        def _(d):
            part_push(r, after(d), z).wait_send()

        @pl.loop(0, levels)
        def _(level):
            @pl.when(has_right & (level <= z))
            def _():
                hop(r, level, 1).wait_send()

            @pl.when(has_left & (level >= z))
            def _():
                hop(r, level, 0).wait_send()

            for j in range(1, group):
                panel_push(r, level, mate(j), i).wait_send()
                term_push(r, level, mate(j), i).wait_send()


def on_device(genotypes, sample_factors, snp_factors, coverage):
    n = lax.axis_size("rows")
    rows, rank = sample_factors.shape
    covered = coverage.shape[1]
    tile = genotypes.shape[1] // covered
    per = covered // n
    own = snp_factors.shape[0] // tile
    width = per * tile
    group = math.gcd(n, 4)
    levels = n // group
    half = own // 2
    st, vt = pl.pallas_call(
        functools.partial(kernel, n, group, per, own, tile),
        out_shape=(
            jax.ShapeDtypeStruct((rank, rows), F32),
            jax.ShapeDtypeStruct((rank, own * tile), F32),
        ),
        in_specs=[
            pl.BlockSpec(memory_space=pltpu.SMEM),
            pl.BlockSpec(memory_space=pl.ANY),
            pl.BlockSpec(memory_space=pltpu.VMEM),
            pl.BlockSpec(memory_space=pltpu.VMEM),
        ],
        out_specs=(
            pl.BlockSpec(memory_space=pltpu.VMEM),
            pl.BlockSpec(memory_space=pltpu.VMEM),
        ),
        scratch_shapes=[
            pltpu.VMEM((n, rows, width), BF16),
            pltpu.VMEM((ROUNDS, n, rank, width), BF16),
            pltpu.VMEM((ROUNDS, n, rank, width), BF16),
            pltpu.VMEM((ROUNDS, n, rank, width), BF16),
            pltpu.VMEM((ROUNDS, n, rank, width), BF16),
            pltpu.VMEM((ROUNDS, levels, half, rank, 2 * tile), BF16),
            pltpu.VMEM((ROUNDS, levels, half, rank, 2 * tile), BF16),
            pltpu.VMEM((ROUNDS, levels, half, rank, 2 * tile), BF16),
            pltpu.VMEM((half, rank, 2 * tile), F32),
            pltpu.VMEM((half, rank, 2 * tile), F32),
            pltpu.VMEM((half, rank, 2 * tile), F32),
            pltpu.VMEM((rank, rows), F32),
            pltpu.VMEM((rank, rows), BF16),
            pltpu.VMEM((rows, rank), F32),
            pltpu.VMEM((rank, rank), F32),
            pltpu.VMEM((own, rank, width), F32),
            pltpu.VMEM((own, width), F32),
            pltpu.SemaphoreType.DMA((n,)),
            pltpu.SemaphoreType.DMA((ROUNDS, n)),
            pltpu.SemaphoreType.DMA((ROUNDS, n)),
            pltpu.SemaphoreType.DMA((ROUNDS, n)),
            pltpu.SemaphoreType.DMA((ROUNDS, n)),
            pltpu.SemaphoreType.DMA((ROUNDS, 2, levels)),
            pltpu.SemaphoreType.DMA((ROUNDS, levels)),
            pltpu.SemaphoreType.DMA((ROUNDS, levels)),
            pltpu.SemaphoreType.DMA((ROUNDS, levels)),
        ],
        compiler_params=pltpu.CompilerParams(
            collective_id=0, has_side_effects=True, vmem_limit_bytes=52 * 1024 * 1024
        ),
    )(coverage, genotypes, sample_factors.T, snp_factors.T)
    return st.T, vt.T


def solution(mesh):
    placed = P(("groups", "rows"), None)
    return jax.shard_map(
        on_device,
        mesh=mesh,
        in_specs=(placed, placed, placed, P("groups", None)),
        out_specs=(placed, placed),
        check_vma=False,
    )
```

```python
import functools
import math

import jax
import jax.numpy as jnp
from jax import lax
from jax.experimental import pallas as pl
from jax.experimental.pallas import tpu as pltpu
from jax.sharding import PartitionSpec as P

ROUNDS = 2
DECAY = 0.02
MESH = pl.DeviceIdType.MESH
F32 = jnp.float32
BF16 = jnp.bfloat16


def nt(a, b):
    return lax.dot_general(a, b, (((1,), (1,)), ((), ())), preferred_element_type=F32)


def nn(a, b):
    return lax.dot_general(a, b, (((1,), (0,)), ((), ())), preferred_element_type=F32)


def three_terms(a):
    hi = a.astype(BF16)
    rest = a - hi.astype(F32)
    mid = rest.astype(BF16)
    low = (rest - mid.astype(F32)).astype(BF16)
    return hi, mid, low


def kernel(n, group, per, own, tile, cov_ref, geno_hbm, st_in, vt_in, st_out, vt_out,
           geno, panels, stage, terms, outgoing, whole, part_out, part_in, pairs, seen, grads,
           st, st_bf, acc, square, total, count,
           geno_sem, panel_send, panel_recv, term_send, term_recv,
           whole_send, whole_recv, part_send, part_recv):
    me = lax.axis_index("rows")
    levels = n // group
    z, i = lax.div(me, group), lax.rem(me, group)
    width = per * tile
    two = 2 * tile
    rank = st.shape[0]
    rows = st.shape[1]

    def at(level, place):
        return level * group + place

    def mate(j):
        return lax.rem(i + j, group)

    def after(d):
        return lax.rem(z + d, levels)

    def before(d):
        return lax.rem(z - d + levels, levels)

    def geno_copy(c):
        return pltpu.make_async_copy(
            geno_hbm.at[:, pl.ds(pl.multiple_of(c * group * width, group * width), group * width)],
            geno.at[c], geno_sem.at[c])

    def remote(src, dst, send, recv, there):
        return pltpu.make_async_remote_copy(
            src_ref=src, dst_ref=dst, send_sem=send, recv_sem=recv,
            device_id={"rows": there}, device_id_type=MESH)

    def hop(r, slot, way):
        return remote(whole.at[r, slot], whole.at[r, slot], whole_send.at[r, way, slot],
                      whole_recv.at[r, slot], at(z - 1 + 2 * way, i))

    has_left, has_right = z > 0, z < levels - 1

    def panel_push(r, level, j, slot):
        return remote(stage.at[r, at(level, j)], panels.at[r, at(level, slot)],
                      panel_send.at[r, at(level, j)], panel_recv.at[r, at(level, slot)], at(z, j))

    def term_push(r, level, j, slot):
        return remote(outgoing.at[r, at(level, j)], terms.at[r, at(level, slot)],
                      term_send.at[r, at(level, j)], term_recv.at[r, at(level, slot)], at(z, j))

    def part_push(r, level, slot):
        return remote(part_out.at[r, level], part_in.at[r, slot], part_send.at[r, level],
                      part_recv.at[r, slot], at(level, i))

    barrier = pltpu.get_barrier_semaphore()

    @pl.loop(1, group)
    def _(j):
        pl.semaphore_signal(barrier, inc=1, device_id={"rows": at(z, mate(j))}, device_id_type=MESH)

    @pl.loop(1, levels)
    def _(d):
        pl.semaphore_signal(barrier, inc=1, device_id={"rows": at(after(d), i)}, device_id_type=MESH)

    @pl.loop(0, levels)
    def _(d):
        geno_copy(before(d)).start()

    st[...] = st_in[...]
    for p in range(own // 2):
        pairs[p] = vt_in[:, p * two:(p + 1) * two]

    def local(b, s, k):
        return jnp.clip(cov_ref[b, s * per + k] - s * own, 0, own - 1)

    def select(level, b):
        def block(k):
            index = local(b, at(level, i), k)
            both = seen[lax.div(index, 2)]
            return jnp.where(lax.rem(index, 2) == 0, both[:, :tile], both[:, tile:])

        return jnp.concatenate([block(k) for k in range(per)], axis=1).astype(BF16)

    place = lax.broadcasted_iota(jnp.int32, (1, width), 1) // tile
    first = lax.broadcasted_iota(jnp.int32, (1, two), 1) < tile

    def listed(b, s):
        out = jnp.full((1, width), local(b, s, 0), jnp.int32)
        for k in range(1, per):
            out = jnp.where(place == k, local(b, s, k), out)
        return out

    count[...] = jnp.zeros_like(count)

    @pl.loop(0, n)
    def _(b):
        row = listed(b, me)
        for c in range(own):
            count[c:c + 1, :] += (row == c).astype(F32)

    pl.semaphore_wait(barrier, group + levels - 2)

    step = 0.5 * math.sqrt(rank) / (n * per * tile)
    for r in range(ROUNDS):
        whole[r, z] = pairs[...].astype(BF16)

        @pl.when(has_right)
        def _():
            hop(r, z, 1).start()

        @pl.when(has_left)
        def _():
            hop(r, z, 0).start()

        def hand_on(level):
            seen[...] = whole[r, level].astype(F32)
            for j in range(1, group):
                stage[r, at(level, mate(j))] = select(level, at(z, mate(j)))
                panel_push(r, level, mate(j), i).start()
            panels[r, at(level, i)] = select(level, me)

        def sample_terms(level):
            for j in range(1, group):
                panel_push(r, level, mate(j), mate(j)).wait_recv()
            if r == 0:
                geno_copy(level).wait()
            panel = jnp.concatenate([panels[r, at(level, j)] for j in range(group)], axis=1)
            acc[...] += nt(geno[level], panel)
            square[...] += nt(panel, panel)

        hand_on(z)
        st_bf[...] = st[...].astype(BF16)
        acc[...] = jnp.zeros_like(acc)

        square[...] = jnp.zeros_like(square)

        @pl.loop(1, levels + 1)
        def _(d):
            @pl.when(z - d >= 0)
            def _():
                hop(r, z - d, 1).wait_recv()

                @pl.when(has_right)
                def _():
                    hop(r, z - d, 1).start()

            @pl.when(z + d < levels)
            def _():
                hop(r, z + d, 0).wait_recv()

                @pl.when(has_left)
                def _():
                    hop(r, z + d, 0).start()

            @pl.when(z - d >= 0)
            def _():
                hand_on(z - d)

            @pl.when(z + d < levels)
            def _():
                hand_on(z + d)

            @pl.when(z - d + 1 >= 0)
            def _():
                sample_terms(z - d + 1)

            @pl.when((d > 1) & (z + d - 1 < levels))
            def _():
                sample_terms(z + d - 1)

        now = st_bf[...]
        fit = sum(nn(part, now) for part in three_terms(square[...]))
        fresh = (1.0 - DECAY) * st[...] + step * (acc[...].T - fit)
        st[...] = fresh
        now = fresh.astype(BF16)
        st_bf[...] = now

        gram = three_terms(nt(now, now))

        def snp_term(s):
            panel = panels[r, s]
            fit = sum(nn(part, panel) for part in gram)
            start = pl.multiple_of(lax.rem(s, group) * width, width)
            seen_geno = geno[lax.div(s, group), :, pl.ds(start, width)]
            return (nn(st_bf[...], seen_geno) - fit).astype(BF16)

        def send_terms(level):
            for j in range(1, group):
                outgoing[r, at(level, mate(j))] = snp_term(at(level, mate(j)))
                term_push(r, level, mate(j), i).start()

        def fold(c):
            out = total[c, :, :two]
            for k in range(1, width // two):
                out = out + total[c, :, k * two:(k + 1) * two]
            return out + pltpu.roll(out, tile, 1)

        def add_up(level):
            owner = at(level, i)
            total[...] = jnp.zeros_like(total)
            for j in range(group):
                if j == 0:
                    value = snp_term(owner)
                else:
                    term_push(r, level, mate(j), mate(j)).wait_recv()
                    value = terms[r, at(level, mate(j))]
                row = listed(at(z, mate(j)), owner)
                wide = value.astype(F32)
                for c in range(own):
                    total[c] += jnp.where(row == c, wide, 0.0)
            return [jnp.where(first, fold(2 * p), fold(2 * p + 1)) for p in range(own // 2)]

        def send_part(level):
            for p, value in enumerate(add_up(level)):
                part_out[r, level, p] = value.astype(BF16)
            part_push(r, level, z).start()

        send_terms(after(1))

        @pl.loop(1, levels)
        def _(d):
            send_terms(after(d + 1))
            send_part(after(d))

        for p, value in enumerate(add_up(z)):
            grads[p] = value

        @pl.loop(1, levels)
        def _(d):
            part_push(r, before(d), before(d)).wait_recv()
            grads[...] += part_in[r, before(d)].astype(F32)

        def rate(c):
            observed = jnp.sum(count[c:c + 1, :], axis=1, keepdims=True) / tile
            return 0.5 * math.sqrt(rank) / (rows * observed)

        for p in range(own // 2):
            pairs[p] = (1.0 - DECAY) * pairs[p] + jnp.where(first, rate(2 * p), rate(2 * p + 1)) * grads[p]

    st_out[...] = st[...]
    for p in range(own // 2):
        vt_out[:, p * two:(p + 1) * two] = pairs[p]

    for r in range(ROUNDS):
        @pl.loop(1, levels)
        def _(d):
            part_push(r, after(d), z).wait_send()

        @pl.loop(0, levels)
        def _(level):
            @pl.when(has_right & (level <= z))
            def _():
                hop(r, level, 1).wait_send()

            @pl.when(has_left & (level >= z))
            def _():
                hop(r, level, 0).wait_send()

            for j in range(1, group):
                panel_push(r, level, mate(j), i).wait_send()
                term_push(r, level, mate(j), i).wait_send()


def on_device(genotypes, sample_factors, snp_factors, coverage):
    n = lax.axis_size("rows")
    rows, rank = sample_factors.shape
    covered = coverage.shape[1]
    tile = genotypes.shape[1] // covered
    per = covered // n
    own = snp_factors.shape[0] // tile
    width = per * tile
    group = math.gcd(n, 4)
    levels = n // group
    half = own // 2
    st, vt = pl.pallas_call(
        functools.partial(kernel, n, group, per, own, tile),
        out_shape=(
            jax.ShapeDtypeStruct((rank, rows), F32),
            jax.ShapeDtypeStruct((rank, own * tile), F32),
        ),
        in_specs=[
            pl.BlockSpec(memory_space=pltpu.SMEM),
            pl.BlockSpec(memory_space=pl.ANY),
            pl.BlockSpec(memory_space=pltpu.VMEM),
            pl.BlockSpec(memory_space=pltpu.VMEM),
        ],
        out_specs=(
            pl.BlockSpec(memory_space=pltpu.VMEM),
            pl.BlockSpec(memory_space=pltpu.VMEM),
        ),
        scratch_shapes=[
            pltpu.VMEM((levels, rows, group * width), BF16),
            pltpu.VMEM((ROUNDS, n, rank, width), BF16),
            pltpu.VMEM((ROUNDS, n, rank, width), BF16),
            pltpu.VMEM((ROUNDS, n, rank, width), BF16),
            pltpu.VMEM((ROUNDS, n, rank, width), BF16),
            pltpu.VMEM((ROUNDS, levels, half, rank, 2 * tile), BF16),
            pltpu.VMEM((ROUNDS, levels, half, rank, 2 * tile), BF16),
            pltpu.VMEM((ROUNDS, levels, half, rank, 2 * tile), BF16),
            pltpu.VMEM((half, rank, 2 * tile), F32),
            pltpu.VMEM((half, rank, 2 * tile), F32),
            pltpu.VMEM((half, rank, 2 * tile), F32),
            pltpu.VMEM((rank, rows), F32),
            pltpu.VMEM((rank, rows), BF16),
            pltpu.VMEM((rows, rank), F32),
            pltpu.VMEM((rank, rank), F32),
            pltpu.VMEM((own, rank, width), F32),
            pltpu.VMEM((own, width), F32),
            pltpu.SemaphoreType.DMA((levels,)),
            pltpu.SemaphoreType.DMA((ROUNDS, n)),
            pltpu.SemaphoreType.DMA((ROUNDS, n)),
            pltpu.SemaphoreType.DMA((ROUNDS, n)),
            pltpu.SemaphoreType.DMA((ROUNDS, n)),
            pltpu.SemaphoreType.DMA((ROUNDS, 2, levels)),
            pltpu.SemaphoreType.DMA((ROUNDS, levels)),
            pltpu.SemaphoreType.DMA((ROUNDS, levels)),
            pltpu.SemaphoreType.DMA((ROUNDS, levels)),
        ],
        compiler_params=pltpu.CompilerParams(
            collective_id=0, has_side_effects=True, vmem_limit_bytes=52 * 1024 * 1024
        ),
    )(coverage, genotypes, sample_factors.T, snp_factors.T)
    return st.T, vt.T


def solution(mesh):
    placed = P(("groups", "rows"), None)
    return jax.shard_map(
        on_device,
        mesh=mesh,
        in_specs=(placed, placed, placed, P("groups", None)),
        out_specs=(placed, placed),
        check_vma=False,
    )
```
